256 devices in a mesh: row: 8 (over z), col: 4 (over y), layer: 8 (over x, core).
Axes of the slice: x: 4, y: 4, z: 8, core: 2. Of those that a mesh axis runs over, the one named last changes fastest.
Arguments:
- fine_operator: bfloat16 [12288, 12288], P('row', ('layer', 'col')), may hold values from -0.0546875 to 0.0546875
- operator_pattern: int32 [192, 192], P('row', ('layer', 'col')), may hold values from 0 to 1
- prolongation: bfloat16 [12288, 4096], P(('layer', 'row'), 'col'), may hold values from -6 to 6
- prolong_pattern: int32 [192, 64], P(('layer', 'row'), 'col'), may hold values from 0 to 1
- restriction: bfloat16 [4096, 12288], P('col', ('row', 'layer')), may hold values from -0.15625 to 0.15625
- restrict_pattern: int32 [64, 192], P('col', ('row', 'layer')), may hold values from 0 to 1
Outputs:
- operator_prolong: bfloat16 [12288, 4096], P(('row', 'layer'), 'col')
- coarse_operator: float32 [4096, 4096], P(('row', 'layer'), 'col')
The draws below stay inside these ranges and needn't reach their ends.
All inputs are finite; a program needn't handle non-finite values.
Results may differ from the reference program's by a relative error of at most 0.0029.
Values may be sent and summed in bfloat16 or wider, within the bound.
No kernel may reach another device: no remote copies, remote signals or barrier semaphores. Data moves between devices by JAX's collectives and lax.ppermute only.
A program may use at most 64 MiB of HBM per device.

```python
import jax
import jax.numpy as jnp

BS = 64
NC = 4096
NF = 12288


def pattern_rows(key, height, breadth):
    key_well, key_density, key_fill = jax.random.split(key, 3)
    well_row = jax.random.randint(key_well, (height, 1), 0, 8) == 0
    density = jnp.where(well_row, 8, jax.random.randint(key_density, (height, 1), 1, 5))
    filled = jax.random.randint(key_fill, (height, breadth), 0, 8) < density
    return filled.astype(jnp.int32)


def draw_operator_pattern(key, part):
    key = jax.random.fold_in(key, 11)
    return pattern_rows(key, NF // BS, NF // BS)


def draw_prolong_pattern(key, part):
    key = jax.random.fold_in(key, 23)
    return pattern_rows(key, NF // BS, NC // BS)


def draw_restrict_pattern(key, part):
    key = jax.random.fold_in(key, 37)
    return pattern_rows(key, NC // BS, NF // BS)


def raised(array, rng, source, target, parts, factor):
    def block_of(dim):
        return (jnp.arange(array.shape[dim]) // (array.shape[dim] // parts)).reshape((-1,) + (1,) * (array.ndim - 1 - dim))

    near = jax.random.permutation(rng, parts)[block_of(target)]
    second = (block_of(target) + parts // 2) % parts
    return jnp.where((block_of(source) == near) | (block_of(source) == second), factor * array, array)


def block_levels(key, dims, shards, low, high):
    level = 1.0
    for position, parts in shards:
        heights = jax.random.uniform(jax.random.fold_in(jax.random.fold_in(key, 6), position), (parts,), jnp.float32, low / len(shards), high / len(shards))
        level = level * jnp.repeat(jnp.exp(heights), dims[position] // parts).reshape((-1,) + (1,) * (len(dims) - 1 - position))
    return level


def scatter_about(key, extent, width, reach, cuts=(), held_as=jnp.bfloat16):
    array = jax.random.normal(key, extent, jnp.float32) * width
    if len(cuts) > 0:
        array = block_levels(key, extent, cuts, -0.22, 0.18) * array
    return jnp.clip(array, min=-reach, max=reach).astype(held_as)


def bell_draw_with(rng, dims, width, most, pieces, heavy, kind=jnp.bfloat16):
    entries = width * jax.random.normal(rng, dims, jnp.float32)
    if pieces:
        entries = entries * block_levels(rng, dims, pieces, -0.22, 0.18)
    return jnp.clip(raised(entries, jax.random.fold_in(rng, 3), *heavy), -most, most).astype(kind)


def setup_inputs(seed: int = 0) -> dict:
    seeds = jax.random.split(jax.random.key(seed), 7)
    fine_operator = scatter_about(seeds[0], (NF, NF), NF ** -0.5, 0.0546875, ((0, 8), (1, 32)))
    operator_pattern = draw_operator_pattern(jax.random.fold_in(seeds[6], 71), 0)
    prolongation = scatter_about(seeds[2], (NF, NC), 1.0, 6.0, ((0, 64), (1, 4)))
    prolong_pattern = draw_prolong_pattern(jax.random.fold_in(seeds[6], 71), 0)
    restriction = bell_draw_with(seeds[4], (NC, NF), NF ** -0.5, 0.15625, ((0, 4), (1, 64)), (1, 0, 64, 4.0))
    restrict_pattern = draw_restrict_pattern(jax.random.fold_in(seeds[6], 71), 0)
    return dict(fine_operator=fine_operator, operator_pattern=operator_pattern, prolongation=prolongation, prolong_pattern=prolong_pattern, restriction=restriction, restrict_pattern=restrict_pattern)


def apply_pattern(values, pattern):
    height, breadth = values.shape
    blocks = values.reshape(height // BS, BS, breadth // BS, BS)
    factor = pattern.astype(values.dtype)[:, None, :, None]
    return (blocks * factor).reshape(height, breadth)


def reference(fine_operator, operator_pattern, prolongation, prolong_pattern, restriction, restrict_pattern):
    masked_operator = apply_pattern(fine_operator, operator_pattern)
    masked_prolong = apply_pattern(prolongation, prolong_pattern)
    masked_restrict = apply_pattern(restriction, restrict_pattern)
    operator_prolong = jnp.dot(masked_operator, masked_prolong, preferred_element_type=jnp.float32).astype(jnp.bfloat16)
    coarse_operator = jnp.dot(masked_restrict, operator_prolong, preferred_element_type=jnp.float32)
    return operator_prolong, coarse_operator
```

```python
import functools

import jax
import jax.numpy as jnp
from jax import lax
from jax.experimental import pallas as pl
from jax.experimental.pallas import tpu as pltpu
from jax.sharding import PartitionSpec as P

BS = 64
BF = jnp.bfloat16
F32 = jnp.float32
NCH = 2
SLOT_X = (2, 1, 3, 0)


def shift(v, axis, step):
    size = lax.axis_size(axis)
    step = step * 2 if axis == "layer" else step
    return lax.ppermute(v, axis, [(i, (i + step) % size) for i in range(size)])


def swap_cores(v):
    size = lax.axis_size("layer")
    return lax.ppermute(v, "layer", [(i, i ^ 1) for i in range(size)])


def dot(a, b):
    return jnp.dot(a, b, preferred_element_type=F32)


def lane_factor(pattern_ref, block_row, first, blocks):
    lane = lax.broadcasted_iota(jnp.int32, (1, blocks * BS), 1) // BS
    row = jnp.zeros((1, blocks * BS), F32)
    for j in range(blocks):
        row = jnp.where(lane == j, pattern_ref[first + j, block_row].astype(F32), row)
    return row.astype(BF)


def mask_operator_kernel(at_ref, pattern_ref, a_ref, o_ref):
    x, c = at_ref[0], at_ref[1]
    for half in range(2):
        core = (1 - c) if half == 0 else c
        for slot in range(4):
            source = (lax.rem(x + SLOT_X[slot], 4) * 2 + core) * 3
            for b in range(3):
                row = pl.multiple_of((source + b) * BS, BS)
                factor = lane_factor(pattern_ref, source + b, 0, 6)
                o_ref[pl.ds(((half * 4 + slot) * 3 + b) * BS, BS), :] = (
                    a_ref[pl.ds(row, BS), :] * factor
                )


def mask_prolong_kernel(pattern_ref, p_ref, o_ref):
    for b in range(3):
        lane = lax.broadcasted_iota(jnp.int32, (1, 1024), 1) // BS
        row = jnp.zeros((1, 1024), F32)
        for j in range(16):
            row = jnp.where(lane == j, pattern_ref[b, j].astype(F32), row)
        rows = slice(b * BS, (b + 1) * BS)
        o_ref[rows, :] = p_ref[rows, :] * row.astype(BF)


def mask_restrict_kernel(pattern_ref, r_ref, o_ref):
    lane = lax.broadcasted_iota(jnp.int32, (1, 128), 1) // BS
    for slot in range(4):
        to = slot
        for zz in range(2):
            block = zz * 8 + to * 2
            column = block * BS
            for b in range(3):
                low = pattern_ref[b, block].astype(F32)
                high = pattern_ref[b, block + 1].astype(F32)
                factor = jnp.where(lane == 0, low, high).astype(BF)
                rows = slice(b * BS, (b + 1) * BS)
                o_ref[slot, rows, zz * 128 : (zz + 1) * 128] = (
                    r_ref[rows, column : column + 128] * factor
                )


SMEM = pl.BlockSpec(memory_space=pltpu.SMEM)
VMEM = pl.BlockSpec(memory_space=pltpu.VMEM)


def local(kernel, shape, specs, name):
    return pl.pallas_call(
        kernel,
        out_shape=jax.ShapeDtypeStruct(shape, BF),
        in_specs=specs,
        out_specs=VMEM,
        name=name,
    )


def after(v, *others):
    return lax.optimization_barrier((v, others))[0]


def from_ring(v, axis):
    return shift(v, axis, 2), shift(v, axis, -1), shift(v, axis, 1), v


def on_device(
    fine_operator, operator_pattern, prolongation, prolong_pattern, restriction, restrict_pattern
):
    layer = lax.axis_index("layer")
    y = lax.axis_index("col")
    z = lax.axis_index("row")
    x, c = layer // 2, layer % 2
    at = jnp.stack([x, c]).astype(jnp.int32)

    a0 = local(mask_operator_kernel, (1536, 384), [SMEM, SMEM, VMEM], "mask_operator")(
        at, operator_pattern.T, fine_operator
    )
    p0 = local(mask_prolong_kernel, (192, 1024), [SMEM, VMEM], "mask_prolong")(
        *after((prolong_pattern, prolongation), a0)
    )
    r0 = local(mask_restrict_kernel, (4, 192, 256), [SMEM, VMEM], "mask_restrict")(
        restrict_pattern.T, restriction.T
    )

    a_left, a_right = shift(a0, "col", 1), shift(a0, "col", -1)

    p_full = jnp.zeros((8, 192, 1024), BF)

    def put(full, block, dz, first=0):
        return lax.dynamic_update_slice(full, block[None], (lax.rem(z + dz + 8, 8), first, 0))

    p_full = put(p_full, p0, 0)
    up, down = p0, p0
    for d in range(1, 4):
        up, down = shift(up, "row", 1), shift(down, "row", -1)
        p_full = put(put(p_full, up, -d), down, d)
        if d == 1:
            r0 = after(r0, up, down)
            size = lax.axis_size("layer")
            groups = [list(range(core, size, 2)) for core in range(2)]
            r_x = lax.all_to_all(r0, "layer", 0, 0, tiled=False, axis_index_groups=groups)
            r_x = jnp.concatenate(
                [
                    lax.dynamic_index_in_dim(r_x, lax.rem(x + slot, 4), 0, keepdims=False)
                    for slot in SLOT_X
                ],
                0,
            )
        if d == 2:
            up, down = after((up, down), r_x)
    p_full = put(p_full, shift(up[:96], "row", 1), -4)
    p_full = put(p_full, shift(down[96:], "row", -1), 4, 96)
    p_full = p_full.reshape(4, 384, 1024)

    def p_of(dy):
        return lax.dynamic_index_in_dim(p_full, lax.rem(y + dy + 4, 4), 0, keepdims=False)

    a_top = shift(a_left[:768], "col", 1)
    a_bottom = shift(a_right[768:], "col", -1)
    a_top = after(a_top, a_bottom)

    r_far, r_right, r_left, r_x = from_ring(after(r_x, a_top, a_bottom), "col")

    acc = dot(a0, p_of(0)) + dot(a_left, p_of(-1)) + dot(a_right, p_of(1))
    p_far = p_of(2)
    width = 1024 // NCH
    outs, coarse = [], []
    for n in range(NCH):
        cols = slice(n * width, (n + 1) * width)
        away = acc[:768, cols] + dot(a_top, p_far[:, cols])
        mine = acc[768:, cols] + dot(a_bottom, p_far[:, cols])
        s = mine + swap_cores(away)
        far, ahead, behind, own = s[:192], s[192:384], s[384:576], s[576:]
        far_top = shift(far[:96], "layer", 1)
        far_bottom = shift(far[96:], "layer", -1)
        ahead = ahead + jnp.pad(far_top, ((0, 96), (0, 0)))
        behind = behind + jnp.pad(far_bottom, ((96, 0), (0, 0)))
        block = (own + shift(ahead, "layer", 1) + shift(behind, "layer", -1)).astype(BF)
        outs.append(block)
        if n == 0:
            r_blocks = after((r_far, r_right, r_left, r_x), block)
            r_full = jnp.zeros((4, 768, 256), BF)
            for piece, dy in zip(r_blocks, (2, 1, 3, 0)):
                r_full = lax.dynamic_update_slice(
                    r_full, piece[None], (lax.rem(y + dy, 4), 0, 0)
                )
            r_full = r_full.transpose(0, 2, 1).reshape(8, 128, 768)
            r_full = lax.dynamic_slice_in_dim(jnp.concatenate([r_full, r_full], 0), z, 8, 0)
            r_full = r_full.reshape(8, 2, 64, 768)
            r_away = lax.dynamic_index_in_dim(r_full, 1 - c, 1, keepdims=False).reshape(512, 768)
            r_mine = lax.dynamic_index_in_dim(r_full, c, 1, keepdims=False).reshape(512, 768)
        b = jnp.concatenate(from_ring(block, "layer"), 0)
        q = dot(r_mine, b) + swap_cores(dot(r_away, b))
        coarse.append(q.reshape(8, 64, width))
    q = jnp.concatenate(coarse, 2)
    q0 = q[0]
    q = lax.dynamic_slice_in_dim(jnp.concatenate([q, q], 0).astype(BF), lax.rem(8 - z, 8), 8, 0)
    q = lax.all_to_all(q, "row", 0, 0, tiled=False)
    q = jnp.where(lax.broadcasted_iota(jnp.int32, q.shape, 0) == z, 0.0, q.astype(F32))
    return jnp.concatenate(outs, 1), q0 + jnp.sum(q, 0)


def solution(mesh):
    placed = (
        P("row", ("layer", "col")),
        P("row", ("layer", "col")),
        P(("layer", "row"), "col"),
        P(("layer", "row"), "col"),
        P("col", ("row", "layer")),
        P("col", ("row", "layer")),
    )
    return jax.shard_map(
        on_device,
        mesh=mesh,
        in_specs=placed,
        out_specs=(P(("row", "layer"), "col"), P(("row", "layer"), "col")),
        check_vma=False,
    )
```

```python
import functools

import jax
import jax.numpy as jnp
from jax import lax
from jax.experimental import pallas as pl
from jax.experimental.pallas import tpu as pltpu
from jax.sharding import PartitionSpec as P

BS = 64
BF = jnp.bfloat16
F32 = jnp.float32
NCH = 2
SLOT_X = (2, 1, 3, 0)


def shift(v, axis, step):
    size = lax.axis_size(axis)
    step = step * 2 if axis == "layer" else step
    return lax.ppermute(v, axis, [(i, (i + step) % size) for i in range(size)])


def swap_cores(v):
    size = lax.axis_size("layer")
    return lax.ppermute(v, "layer", [(i, i ^ 1) for i in range(size)])


def dot(a, b):
    return jnp.dot(a, b, preferred_element_type=F32)


def mask_kernel(at_ref, a_pattern_ref, p_pattern_ref, a_ref, p_ref, a_out_ref, p_out_ref):
    lane = lax.broadcasted_iota(jnp.int32, (1, 128), 1) // BS

    def factor(low, high):
        return jnp.where(lane == 0, low.astype(F32), high.astype(F32)).astype(BF)

    x, c = at_ref[0] // 2, lax.rem(at_ref[0], 2)
    for half in range(2):
        core = (1 - c) if half == 0 else c
        for slot in range(4):
            source = (lax.rem(x + SLOT_X[slot], 4) * 2 + core) * 3
            for b in range(3):
                block = source + b
                rows = pl.ds(pl.multiple_of(block * BS, BS), BS)
                first = ((half * 4 + slot) * 3 + b) * BS
                for j in range(3):
                    cols = slice(j * 128, (j + 1) * 128)
                    a_out_ref[first : first + BS, cols] = a_ref[rows, cols] * factor(
                        a_pattern_ref[2 * j, block], a_pattern_ref[2 * j + 1, block]
                    )
    for b in range(3):
        rows = slice(b * BS, (b + 1) * BS)
        for j in range(8):
            cols = slice(j * 128, (j + 1) * 128)
            p_out_ref[rows, cols] = p_ref[rows, cols] * factor(
                p_pattern_ref[b, 2 * j], p_pattern_ref[b, 2 * j + 1]
            )


def mask_restrict_kernel(at_ref, pattern_ref, r_ref, *o_refs):
    lane = lax.broadcasted_iota(jnp.int32, (1, 128), 1) // BS
    for slot, o_ref in zip(SLOT_X, o_refs):
        to = lax.rem(at_ref[0] // 2 + 4 - slot, 4)
        for zz in range(2):
            block = zz * 8 + to * 2
            column = pl.multiple_of(block * BS, 128)
            for b in range(3):
                low = pattern_ref[b, block].astype(F32)
                high = pattern_ref[b, block + 1].astype(F32)
                factor = jnp.where(lane == 0, low, high).astype(BF)
                rows = slice(b * BS, (b + 1) * BS)
                o_ref[rows, zz * 128 : (zz + 1) * 128] = (
                    r_ref[rows, pl.ds(column, 128)] * factor
                )


SMEM = pl.BlockSpec(memory_space=pltpu.SMEM)
VMEM = pl.BlockSpec(memory_space=pltpu.VMEM)


def after(v, *others):
    return lax.optimization_barrier((v, others))[0]


def from_ring(v, axis):
    return shift(v, axis, 2), shift(v, axis, -1), shift(v, axis, 1), v


def on_device(
    fine_operator, operator_pattern, prolongation, prolong_pattern, restriction, restrict_pattern
):
    layer = lax.axis_index("layer")
    y = lax.axis_index("col")
    z = lax.axis_index("row")
    x, c = layer // 2, layer % 2
    at = layer[None].astype(jnp.int32)

    a0, p0 = pl.pallas_call(
        mask_kernel,
        out_shape=[
            jax.ShapeDtypeStruct((1536, 384), BF),
            jax.ShapeDtypeStruct((192, 1024), BF),
        ],
        in_specs=[SMEM, SMEM, SMEM, VMEM, VMEM],
        out_specs=[VMEM, VMEM],
        name="mask",
    )(at, operator_pattern.T, prolong_pattern, fine_operator, prolongation)
    r0 = pl.pallas_call(
        mask_restrict_kernel,
        out_shape=[jax.ShapeDtypeStruct((192, 256), BF)] * 4,
        in_specs=[SMEM, SMEM, VMEM],
        out_specs=[VMEM] * 4,
        name="mask_restrict",
    )(*after((at, restrict_pattern.T, restriction.T), p0))

    a_left, a_right = shift(a0, "col", 1), shift(a0, "col", -1)

    p_full = jnp.zeros((8, 192, 1024), BF)

    def put(full, block, dz, first=0):
        return lax.dynamic_update_slice(full, block[None], (lax.rem(z + dz + 8, 8), first, 0))

    p_full = put(p_full, p0, 0)
    r_x = []
    up, down = p0, p0
    for d in range(1, 4):
        r_x.append(shift(after(r0[d - 1], up, down), "layer", -SLOT_X[d - 1]))
        if d > 1:
            up, down, r_x[d - 2] = after((up, down, r_x[d - 2]), r_x[d - 2])
        up, down = shift(up, "row", 1), shift(down, "row", -1)
        p_full = put(put(p_full, up, -d), down, d)
        if d == 2:
            up, down = after((up, down), a_left, a_right)
            a_top = shift(a_left[:768], "col", 1)
            a_bottom = shift(a_right[768:], "col", -1)
    up, down, r_x[2] = after((up, down, r_x[2]), r_x[2])
    r_x = jnp.concatenate(r_x + [r0[3]], 0)
    p_full = put(p_full, shift(up[:96], "row", 1), -4)
    p_full = put(p_full, shift(down[96:], "row", -1), 4, 96)
    p_full = p_full.reshape(4, 384, 1024)

    def p_of(dy):
        return lax.dynamic_index_in_dim(p_full, lax.rem(y + dy + 4, 4), 0, keepdims=False)

    a_top = after(a_top, a_bottom)

    acc = dot(a0, p_of(0)) + dot(a_left, p_of(-1))
    acc = acc + dot(a_right, p_of(1))
    p_far = p_of(2)
    width = 1024 // NCH
    outs, coarse = [], []
    for n in range(NCH):
        cols = slice(n * width, (n + 1) * width)
        away = acc[:768, cols] + dot(a_top, p_far[:, cols])
        mine = acc[768:, cols] + dot(a_bottom, p_far[:, cols])
        s = mine + swap_cores(away)
        if n == 0:
            r_full = jnp.broadcast_to(after(r_x, s), (4, 768, 256))
            r_full = lax.all_to_all(r_full, "col", 0, 0)
        far, ahead, behind, own = s[:192], s[192:384], s[384:576], s[576:]
        parts = after(
            (
                shift(ahead, "layer", 1),
                shift(behind, "layer", -1),
                shift(far.astype(BF), "layer", 2),
            )
        )
        block = (own + parts[0] + parts[1] + parts[2].astype(F32)).astype(BF)
        outs.append(block)
    r_full = r_full.transpose(0, 2, 1).reshape(8, 128, 768)
    r_full = lax.dynamic_slice_in_dim(jnp.concatenate([r_full, r_full], 0), z, 8, 0)
    r_full = r_full.reshape(8, 2, 64, 768)
    r_away = lax.dynamic_index_in_dim(r_full, 1 - c, 1, keepdims=False).reshape(512, 768)
    r_mine = lax.dynamic_index_in_dim(r_full, c, 1, keepdims=False).reshape(512, 768)
    for block in outs:
        b = jnp.concatenate(from_ring(block, "layer"), 0)
        q = dot(r_mine, b) + swap_cores(dot(r_away, b))
        coarse.append(q.reshape(8, 64, width))
    q = jnp.concatenate(coarse, 2)
    sent = q.astype(BF)
    total = q[0]
    for block in after(tuple(shift(sent[d], "row", d) for d in (4, 3, 5, 2, 6, 1, 7))):
        total = total + block.astype(F32)
    return jnp.concatenate(outs, 1), total


def solution(mesh):
    placed = (
        P("row", ("layer", "col")),
        P("row", ("layer", "col")),
        P(("layer", "row"), "col"),
        P(("layer", "row"), "col"),
        P("col", ("row", "layer")),
        P("col", ("row", "layer")),
    )
    return jax.shard_map(
        on_device,
        mesh=mesh,
        in_specs=placed,
        out_specs=(P(("row", "layer"), "col"), P(("row", "layer"), "col")),
        check_vma=False,
    )
```

```python
import functools

import jax
import jax.numpy as jnp
from jax import lax
from jax.experimental import pallas as pl
from jax.experimental.pallas import tpu as pltpu
from jax.sharding import PartitionSpec as P

BS = 64
BF = jnp.bfloat16
F32 = jnp.float32
NCH = 2
SLOT_X = (2, 1, 3, 0)


def shift(v, axis, step):
    size = lax.axis_size(axis)
    step = step * 2 if axis == "layer" else step
    return lax.ppermute(v, axis, [(i, (i + step) % size) for i in range(size)])


def swap_cores(v):
    size = lax.axis_size("layer")
    return lax.ppermute(v, "layer", [(i, i ^ 1) for i in range(size)])


def dot(a, b):
    return jnp.dot(a, b, preferred_element_type=F32)


def mask_kernel(at_ref, a_pattern_ref, p_pattern_ref, a_ref, p_ref, a_out_ref, p_out_ref):
    lane = lax.broadcasted_iota(jnp.int32, (1, 128), 1) // BS

    def factor(low, high):
        return jnp.where(lane == 0, low.astype(F32), high.astype(F32)).astype(BF)

    x, c = at_ref[0] // 2, lax.rem(at_ref[0], 2)
    for half in range(2):
        core = (1 - c) if half == 0 else c
        for slot in range(4):
            source = (lax.rem(x + SLOT_X[slot], 4) * 2 + core) * 3
            for b in range(3):
                block = source + b
                rows = pl.ds(pl.multiple_of(block * BS, BS), BS)
                first = ((half * 4 + slot) * 3 + b) * BS
                for j in range(3):
                    cols = slice(j * 128, (j + 1) * 128)
                    a_out_ref[first : first + BS, cols] = a_ref[rows, cols] * factor(
                        a_pattern_ref[2 * j, block], a_pattern_ref[2 * j + 1, block]
                    )
    for b in range(3):
        rows = slice(b * BS, (b + 1) * BS)
        for j in range(8):
            cols = slice(j * 128, (j + 1) * 128)
            p_out_ref[rows, cols] = p_ref[rows, cols] * factor(
                p_pattern_ref[b, 2 * j], p_pattern_ref[b, 2 * j + 1]
            )


def mask_restrict_kernel(at_ref, pattern_ref, r_ref, *o_refs):
    lane = lax.broadcasted_iota(jnp.int32, (1, 128), 1) // BS
    for slot, o_ref in zip(SLOT_X, o_refs):
        to = lax.rem(at_ref[0] // 2 + 4 - slot, 4)
        for zz in range(2):
            block = zz * 8 + to * 2
            column = pl.multiple_of(block * BS, 128)
            for b in range(3):
                low = pattern_ref[b, block].astype(F32)
                high = pattern_ref[b, block + 1].astype(F32)
                factor = jnp.where(lane == 0, low, high).astype(BF)
                rows = slice(b * BS, (b + 1) * BS)
                o_ref[rows, zz * 128 : (zz + 1) * 128] = (
                    r_ref[rows, pl.ds(column, 128)] * factor
                )


SMEM = pl.BlockSpec(memory_space=pltpu.SMEM)
VMEM = pl.BlockSpec(memory_space=pltpu.VMEM)


def after(v, *others):
    return lax.optimization_barrier((v, others))[0]


def from_ring(v, axis):
    return shift(v, axis, -1), shift(v, axis, 1), shift(v, axis, 2), v


def on_device(
    fine_operator, operator_pattern, prolongation, prolong_pattern, restriction, restrict_pattern
):
    layer = lax.axis_index("layer")
    y = lax.axis_index("col")
    z = lax.axis_index("row")
    x, c = layer // 2, layer % 2
    at = layer[None].astype(jnp.int32)

    a0, p0 = pl.pallas_call(
        mask_kernel,
        out_shape=[
            jax.ShapeDtypeStruct((1536, 384), BF),
            jax.ShapeDtypeStruct((192, 1024), BF),
        ],
        in_specs=[SMEM, SMEM, SMEM, VMEM, VMEM],
        out_specs=[VMEM, VMEM],
        name="mask",
    )(at, operator_pattern.T, prolong_pattern, fine_operator, prolongation)
    r0 = pl.pallas_call(
        mask_restrict_kernel,
        out_shape=[jax.ShapeDtypeStruct((192, 256), BF)] * 4,
        in_specs=[SMEM, SMEM, VMEM],
        out_specs=[VMEM] * 4,
        name="mask_restrict",
    )(*after((at, restrict_pattern.T, restriction.T), p0))

    a_left, a_right = shift(a0, "col", 1), shift(a0, "col", -1)

    p_full = jnp.zeros((8, 192, 1024), BF)

    def put(full, block, dz, first=0):
        return lax.dynamic_update_slice(full, block[None], (lax.rem(z + dz + 8, 8), first, 0))

    p_full = put(p_full, p0, 0)
    r_x = []
    up, down = p0, p0
    for d in range(1, 4):
        r_x.append(shift(after(r0[d - 1], up, down), "layer", -SLOT_X[d - 1]))
        if d > 1:
            up, down, r_x[d - 2] = after((up, down, r_x[d - 2]), r_x[d - 2])
        up, down = shift(up, "row", 1), shift(down, "row", -1)
        p_full = put(put(p_full, up, -d), down, d)
        if d == 2:
            up, down = after((up, down), a_left, a_right)
            a_top = shift(a_left[:768], "col", 1)
            a_bottom = shift(a_right[768:], "col", -1)
    up, down, r_x[2] = after((up, down, r_x[2]), r_x[2])
    r_x = jnp.concatenate([r_x[1], r_x[2], r_x[0], r0[3]], 0)
    p_full = put(p_full, shift(up[:96], "row", 1), -4)
    p_full = put(p_full, shift(down[96:], "row", -1), 4, 96)
    p_full = p_full.reshape(4, 384, 1024)

    def p_of(dy):
        return lax.dynamic_index_in_dim(p_full, lax.rem(y + dy + 4, 4), 0, keepdims=False)

    a_top = after(a_top, a_bottom)

    acc = dot(a0, p_of(0)) + dot(a_left, p_of(-1))
    acc = acc + dot(a_right, p_of(1))
    p_far = p_of(2)
    width = 1024 // NCH
    outs, coarse = [], []
    for n in range(NCH):
        cols = slice(n * width, (n + 1) * width)
        away = acc[:768, cols] + dot(a_top, p_far[:, cols])
        mine = acc[768:, cols] + dot(a_bottom, p_far[:, cols])
        s = mine + swap_cores(away)
        if n == 0:
            r_full = jnp.broadcast_to(after(r_x, s), (4, 768, 256))
            r_full = lax.all_to_all(r_full, "col", 0, 0)
        far, ahead, behind, own = s[:192], s[192:384], s[384:576], s[576:]
        parts = after(
            (
                shift(ahead, "layer", 1),
                shift(behind, "layer", -1),
                shift(far.astype(BF), "layer", 2),
            )
        )
        block = (own + parts[0] + parts[1] + parts[2].astype(F32)).astype(BF)
        outs.append(block)
    r_full = r_full.transpose(0, 2, 1).reshape(8, 128, 768)
    r_full = lax.dynamic_slice_in_dim(jnp.concatenate([r_full, r_full], 0), z, 8, 0)
    r_full = r_full.reshape(8, 2, 64, 768)
    r_away = lax.dynamic_index_in_dim(r_full, 1 - c, 1, keepdims=False).reshape(512, 768)
    r_mine = lax.dynamic_index_in_dim(r_full, c, 1, keepdims=False).reshape(512, 768)
    for block in outs:
        b = jnp.concatenate(from_ring(block, "layer"), 0)
        q = dot(r_mine, b) + swap_cores(dot(r_away, b))
        coarse.append(q.reshape(8, 64, width))
    q = jnp.concatenate(coarse, 2)
    sent = q.astype(BF)
    total = q[0]
    for block in after(tuple(shift(sent[d], "row", d) for d in (4, 3, 5, 2, 6, 1, 7))):
        total = total + block.astype(F32)
    return jnp.concatenate(outs, 1), total


def solution(mesh):
    placed = (
        P("row", ("layer", "col")),
        P("row", ("layer", "col")),
        P(("layer", "row"), "col"),
        P(("layer", "row"), "col"),
        P("col", ("row", "layer")),
        P("col", ("row", "layer")),
    )
    return jax.shard_map(
        on_device,
        mesh=mesh,
        in_specs=placed,
        out_specs=(P(("row", "layer"), "col"), P(("row", "layer"), "col")),
        check_vma=False,
    )
```

```python
import functools

import jax
import jax.numpy as jnp
from jax import lax
from jax.experimental import pallas as pl
from jax.experimental.pallas import tpu as pltpu
from jax.sharding import PartitionSpec as P

BS = 64
BF = jnp.bfloat16
F32 = jnp.float32
NCH = 2
SLOT_X = (2, 1, 3, 0)


def shift(v, axis, step):
    size = lax.axis_size(axis)
    step = step * 2 if axis == "layer" else step
    return lax.ppermute(v, axis, [(i, (i + step) % size) for i in range(size)])


def swap_cores(v):
    size = lax.axis_size("layer")
    return lax.ppermute(v, "layer", [(i, i ^ 1) for i in range(size)])


def dot(a, b):
    return jnp.dot(a, b, preferred_element_type=F32)


def mask_kernel(at_ref, a_pattern_ref, p_pattern_ref, a_ref, p_ref, a_out_ref, p_out_ref):
    lane = lax.broadcasted_iota(jnp.int32, (1, 128), 1) // BS

    def factor(low, high):
        return jnp.where(lane == 0, low.astype(F32), high.astype(F32)).astype(BF)

    x, c = at_ref[0] // 2, lax.rem(at_ref[0], 2)
    for half in range(2):
        core = (1 - c) if half == 0 else c
        for slot in range(4):
            source = (lax.rem(x + SLOT_X[slot], 4) * 2 + core) * 3
            for b in range(3):
                block = source + b
                rows = pl.ds(pl.multiple_of(block * BS, BS), BS)
                first = ((half * 4 + slot) * 3 + b) * BS
                for j in range(3):
                    cols = slice(j * 128, (j + 1) * 128)
                    a_out_ref[first : first + BS, cols] = a_ref[rows, cols] * factor(
                        a_pattern_ref[2 * j, block], a_pattern_ref[2 * j + 1, block]
                    )
    for b in range(3):
        rows = slice(b * BS, (b + 1) * BS)
        for j in range(8):
            cols = slice(j * 128, (j + 1) * 128)
            p_out_ref[rows, cols] = p_ref[rows, cols] * factor(
                p_pattern_ref[b, 2 * j], p_pattern_ref[b, 2 * j + 1]
            )


def mask_restrict_kernel(at_ref, pattern_ref, r_ref, *o_refs):
    lane = lax.broadcasted_iota(jnp.int32, (1, 128), 1) // BS
    for slot, o_ref in zip(SLOT_X, o_refs):
        to = lax.rem(at_ref[0] // 2 + 4 - slot, 4)
        for zz in range(2):
            block = zz * 8 + to * 2
            column = pl.multiple_of(block * BS, 128)
            for b in range(3):
                low = pattern_ref[b, block].astype(F32)
                high = pattern_ref[b, block + 1].astype(F32)
                factor = jnp.where(lane == 0, low, high).astype(BF)
                rows = slice(b * BS, (b + 1) * BS)
                o_ref[rows, zz * 128 : (zz + 1) * 128] = (
                    r_ref[rows, pl.ds(column, 128)] * factor
                )


SMEM = pl.BlockSpec(memory_space=pltpu.SMEM)
VMEM = pl.BlockSpec(memory_space=pltpu.VMEM)


def after(v, *others):
    return lax.optimization_barrier((v, others))[0]


def from_ring(v, axis):
    return shift(v, axis, -1), shift(v, axis, 1), shift(v, axis, 2), v


def on_device(
    fine_operator, operator_pattern, prolongation, prolong_pattern, restriction, restrict_pattern
):
    layer = lax.axis_index("layer")
    y = lax.axis_index("col")
    z = lax.axis_index("row")
    x, c = layer // 2, layer % 2
    at = layer[None].astype(jnp.int32)

    a0, p0 = pl.pallas_call(
        mask_kernel,
        out_shape=[
            jax.ShapeDtypeStruct((1536, 384), BF),
            jax.ShapeDtypeStruct((192, 1024), BF),
        ],
        in_specs=[SMEM, SMEM, SMEM, VMEM, VMEM],
        out_specs=[VMEM, VMEM],
        name="mask",
    )(at, operator_pattern.T, prolong_pattern, fine_operator, prolongation)
    r0 = pl.pallas_call(
        mask_restrict_kernel,
        out_shape=[jax.ShapeDtypeStruct((192, 256), BF)] * 4,
        in_specs=[SMEM, SMEM, VMEM],
        out_specs=[VMEM] * 4,
        name="mask_restrict",
    )(*after((at, restrict_pattern.T, restriction.T), p0))

    a_left, a_right = shift(a0, "col", 1), shift(a0, "col", -1)

    p_full = jnp.zeros((8, 192, 1024), BF)

    def put(full, block, dz, first=0):
        return lax.dynamic_update_slice(full, block[None], (lax.rem(z + dz + 8, 8), first, 0))

    p_full = put(p_full, p0, 0)
    r_x = []
    up, down = p0, p0
    for d in range(1, 4):
        r_x.append(shift(after(r0[d - 1], up, down), "layer", -SLOT_X[d - 1]))
        if d > 1:
            up, down, r_x[d - 2] = after((up, down, r_x[d - 2]), r_x[d - 2])
        up, down = shift(up, "row", 1), shift(down, "row", -1)
        p_full = put(put(p_full, up, -d), down, d)
        if d == 2:
            up, down = after((up, down), a_left, a_right)
            a_top = shift(a_left[:768], "col", 1)
            a_bottom = shift(a_right[768:], "col", -1)
    up, down, r_x[2] = after((up, down, r_x[2]), r_x[2])
    r_x = jnp.concatenate([r_x[1], r_x[2], r_x[0], r0[3]], 0)
    p_full = put(p_full, shift(up[:96], "row", 1), -4)
    p_full = put(p_full, shift(down[96:], "row", -1), 4, 96)
    p_full = p_full.reshape(4, 384, 1024)

    def p_of(dy):
        return lax.dynamic_index_in_dim(p_full, lax.rem(y + dy + 4, 4), 0, keepdims=False)

    a_top = after(a_top, a_bottom)

    acc = dot(a0, p_of(0)) + dot(a_left, p_of(-1))
    acc = acc + dot(a_right, p_of(1))
    p_far = p_of(2)
    width = 1024 // NCH
    outs, coarse = [], []
    for n in range(NCH):
        cols = slice(n * width, (n + 1) * width)
        away = acc[:768, cols] + dot(a_top, p_far[:, cols])
        mine = acc[768:, cols] + dot(a_bottom, p_far[:, cols])
        s = mine + swap_cores(away)
        if n == 0:
            r_full = jnp.broadcast_to(after(r_x, s), (4, 768, 256))
            r_full = lax.all_to_all(r_full, "col", 0, 0)
        far, ahead, behind, own = s[:192], s[192:384], s[384:576], s[576:]
        parts = after(
            (
                shift(ahead, "layer", 1),
                shift(behind, "layer", -1),
                shift(far.astype(BF), "layer", 2),
            )
        )
        block = (own + parts[0] + parts[1] + parts[2].astype(F32)).astype(BF)
        outs.append(block)
    r_full = r_full.transpose(0, 2, 1).reshape(8, 128, 768)
    r_full = lax.dynamic_slice_in_dim(jnp.concatenate([r_full, r_full], 0), z, 8, 0)
    r_full = r_full.reshape(8, 2, 64, 768)
    r_away = lax.dynamic_index_in_dim(r_full, 1 - c, 1, keepdims=False).reshape(512, 768)
    r_mine = lax.dynamic_index_in_dim(r_full, c, 1, keepdims=False).reshape(512, 768)
    for block in outs:
        b = jnp.concatenate(from_ring(block, "layer"), 0)
        q = dot(r_mine, b) + swap_cores(dot(r_away, b))
        coarse.append(q.reshape(8, 64, width))
    q = jnp.concatenate(coarse, 2)
    q0 = q[0]
    q = lax.dynamic_slice_in_dim(jnp.concatenate([q, q], 0).astype(BF), lax.rem(8 - z, 8), 8, 0)
    q = lax.all_to_all(q, "row", 0, 0, tiled=False)
    q = jnp.where(lax.broadcasted_iota(jnp.int32, q.shape, 0) == z, 0.0, q.astype(F32))
    return jnp.concatenate(outs, 1), q0 + jnp.sum(q, 0)


def solution(mesh):
    placed = (
        P("row", ("layer", "col")),
        P("row", ("layer", "col")),
        P(("layer", "row"), "col"),
        P(("layer", "row"), "col"),
        P("col", ("row", "layer")),
        P("col", ("row", "layer")),
    )
    return jax.shard_map(
        on_device,
        mesh=mesh,
        in_specs=placed,
        out_specs=(P(("row", "layer"), "col"), P(("row", "layer"), "col")),
        check_vma=False,
    )
```
